32 devices in a mesh: ctx: 8 (over y, x, core), mp: 4 (over z).
Axes of the slice: x: 2, y: 2, z: 4, core: 2. Of those that a mesh axis runs over, the one named last changes fastest.
Arguments:
- tokens: bfloat16 [8192, 4096], P('ctx'), may hold values from -6 to 6
- norm_gain: float32 [4096], replicated, may hold values from 0.5 to 1.5
- w_qkv: bfloat16 [4096, 3, 2048], P(None, None, 'mp'), may hold values from -0.25 to 0.25
- conv_filter: float32 [7, 3, 2048], P(None, None, 'mp'), may hold values from -4 to 4
- w_out: bfloat16 [2048, 4096], P('mp'), may hold values from -0.1875 to 0.1875
- contig_offsets: int32 [8192], P('ctx'), may hold values from 0 to 7167, as said below
Outputs:
- block_out: bfloat16 [8192, 4096], P('ctx', 'mp')
The draws below stay inside these ranges and needn't reach their ends.
Inputs may be any that keep to these rules, and one draw needn't show every extreme that they name: `contig_offsets`: 0 where a contig begins, else one more than the previous token's value; the longest contig has 7168 tokens.
All inputs are finite; a program needn't handle non-finite values.
Results may differ from the reference program's by a relative error of at most 0.024.
The reference program's roundings to bfloat16 on the way count: a program that leaves them out, or rounds other values in their place, can miss the bound.
Values may be sent and summed in bfloat16 or wider, within the bound.
No kernel may reach another device: no remote copies, remote signals or barrier semaphores. Data moves between devices by JAX's collectives and lax.ppermute only.
A program may use at most 128 MiB of HBM per device.

```python
import math
import jax
import jax.numpy as jnp
from jax import lax

D = 4096
HEADS = 16
HD = 128
KERNEL = 7
TOK_DEV = 1024
TOKENS = 8192


def draw_w_qkv(key, part):
    key = jax.random.fold_in(key, 11)
    first, second, third = jax.random.split(key, 3)
    channels = HEADS * HD
    unit_scale = 1.0 / math.sqrt(D)
    query_part = jax.random.normal(first, (D, channels), jnp.float32) * unit_scale
    key_part = jax.random.normal(second, (D, channels), jnp.float32) * unit_scale
    value_part = jax.random.normal(third, (D, channels), jnp.float32) * unit_scale
    stacked = jnp.stack([query_part, key_part, value_part], axis=1)
    return jnp.clip(stacked, -0.25, 0.25).astype(jnp.bfloat16)


def draw_contig_offsets(key, part):
    key = jax.random.fold_in(key, 5)
    first, second = jax.random.split(key, 2)
    positions = jnp.arange(TOKENS, dtype=jnp.int32)
    long_length = TOKENS - TOK_DEV
    long_begin = jax.random.randint(first, (), 0, TOK_DEV + 1, dtype=jnp.int32)
    starts = jax.random.randint(second, (TOKENS,), 0, 32, dtype=jnp.int32) == 0
    inside_long = (positions > long_begin) & (positions < long_begin + long_length)
    starts = starts & jnp.logical_not(inside_long) | (positions == long_begin) | (positions == long_begin + long_length) | (positions == 0)
    latest = lax.cummax(jnp.where(starts, positions, 0), axis=0)
    return (positions - latest).astype(jnp.int32)


def raised(entries, rng, source, target, blocks, factor):
    def block_of(dim):
        return (jnp.arange(entries.shape[dim]) // (entries.shape[dim] // blocks)).reshape((-1,) + (1,) * (entries.ndim - 1 - dim))

    one_side = jax.random.permutation(rng, blocks)[block_of(target)]
    far = (block_of(target) + blocks // 2) % blocks
    return jnp.where((block_of(source) == one_side) | (block_of(source) == far), factor * entries, entries)


def levels(own_key, extent, cuts, low, high):
    gain = 1.0
    for axis_at, parts in cuts:
        draws = jax.random.uniform(jax.random.fold_in(jax.random.fold_in(own_key, 6), axis_at), (parts,), jnp.float32, low / len(cuts), high / len(cuts))
        gain = gain * jnp.repeat(jnp.exp(draws), extent[axis_at] // parts).reshape((-1,) + (1,) * (len(extent) - 1 - axis_at))
    return gain


def scatter_about(key, shape, spread, limit, cuts=(), kind=jnp.bfloat16):
    loudness = levels(key, shape, cuts, -0.22, 0.18) if cuts else 1.0
    values = jax.random.normal(key, shape, jnp.float32) * spread * loudness
    return jnp.minimum(jnp.maximum(values, -limit), limit).astype(kind)


def gaussian_with(stream_key, extent, width, reach, cuts, heavy, held_as=jnp.bfloat16):
    entries = width * jax.random.normal(stream_key, extent, jnp.float32)
    if cuts:
        entries = entries * levels(stream_key, extent, cuts, -0.22, 0.18)
    return jnp.clip(raised(entries, jax.random.fold_in(stream_key, 3), *heavy), -reach, reach).astype(held_as)


def setup_inputs(seed: int = 0) -> dict:
    splits = jax.random.split(jax.random.key(seed), 7)
    tokens = scatter_about(splits[0], (TOKENS, D), 1.0, 6.0, ((0, 8),))
    norm_gain = jnp.clip(1.0 + 0.1 * jax.random.normal(splits[1], (D,), jnp.float32), 0.5, 1.5)
    w_qkv = draw_w_qkv(jax.random.fold_in(splits[6], 71), 0)
    conv_filter = scatter_about(splits[3], (KERNEL, 3, HEADS * HD), 0.8, 4.0, ((2, 4),), jnp.float32)
    w_out = gaussian_with(splits[4], (HEADS * HD, D), (HEADS * HD) ** -0.5, 0.1875, ((0, 4),), (0, 1, 4, 2.0))
    contig_offsets = draw_contig_offsets(jax.random.fold_in(splits[6], 71), 0)
    return {"tokens": tokens, "norm_gain": norm_gain, "w_qkv": w_qkv, "conv_filter": conv_filter, "w_out": w_out, "contig_offsets": contig_offsets}


def normalize(tokens, norm_gain):
    tokens_float = tokens.astype(jnp.float32)
    inverse = lax.rsqrt(lax.optimization_barrier(jnp.mean(tokens_float * tokens_float, axis=-1, keepdims=True)) + 1e-06)
    return (tokens_float, (tokens_float * inverse * norm_gain).astype(jnp.bfloat16))

def short_filter(projected, history, conv_filter, contig_offsets):
    rows_here = projected.shape[0]
    padded = jnp.concatenate([history, projected], axis=0)
    filtered = jnp.zeros(projected.shape, jnp.float32)
    for lag_step in range(KERNEL):
        begin_row = KERNEL - 1 - lag_step
        shifted = padded[begin_row:begin_row + rows_here].astype(jnp.float32)
        usable = (contig_offsets >= lag_step)[:, None, None]
        filtered = filtered + jnp.where(usable, conv_filter[lag_step] * shifted, 0.0)
    return filtered.astype(jnp.bfloat16)

def reference(tokens, norm_gain, w_qkv, conv_filter, w_out, contig_offsets):
    tokens_float, normed = normalize(tokens, norm_gain)
    channels = HEADS * HD
    projected = jnp.dot(normed, w_qkv.reshape(D, 3 * channels), preferred_element_type=jnp.float32)
    projected = projected.astype(jnp.bfloat16).reshape(TOKENS, 3, channels)
    history = jnp.zeros((KERNEL - 1, 3, channels), jnp.bfloat16)
    mixed_qkv = short_filter(projected, history, conv_filter, contig_offsets)
    queries = mixed_qkv[:, 0].reshape(TOKENS, HEADS, HD).transpose(1, 0, 2)
    key_rows = mixed_qkv[:, 1].reshape(TOKENS, HEADS, HD).transpose(1, 0, 2)
    val_rows = mixed_qkv[:, 2].reshape(TOKENS, HEADS, HD).transpose(1, 0, 2)
    positions = jnp.arange(TOKENS, dtype=jnp.int32)
    contig_first = positions - contig_offsets
    score_scale = 1.0 / math.sqrt(HD)
    pieces = []
    for block_index in range(TOKENS // TOK_DEV):
        row_low = block_index * TOK_DEV
        row_high = row_low + TOK_DEV
        query_pos = positions[row_low:row_high]
        first_here = contig_first[row_low:row_high]
        key_pos = positions[:row_high]
        allowed = (key_pos[None, :] <= query_pos[:, None]) & (key_pos[None, :] >= first_here[:, None])

        def one_head(operands, allowed=allowed):
            query_head, key_head, value_head = operands
            scores = jnp.dot(query_head, key_head.T, preferred_element_type=jnp.float32) * score_scale
            row_max = lax.optimization_barrier(jnp.max(jnp.where(allowed, scores, -jnp.inf), axis=-1, keepdims=True))
            weights = jnp.where(allowed, jnp.exp(scores - row_max), 0.0)
            total = lax.optimization_barrier(jnp.sum(weights, axis=-1, keepdims=True))
            mixed = jnp.dot(weights.astype(jnp.bfloat16), value_head, preferred_element_type=jnp.float32)
            return mixed / total
        attended = lax.map(one_head, (queries[:, row_low:row_high], key_rows[:, :row_high], val_rows[:, :row_high]))
        pieces.append(attended.transpose(1, 0, 2).reshape(TOK_DEV, channels).astype(jnp.bfloat16))
    attended_all = jnp.concatenate(pieces, axis=0)
    projected_out = jnp.dot(attended_all, w_out, preferred_element_type=jnp.float32)
    return (tokens_float + projected_out).astype(jnp.bfloat16)
```

```python
import functools
import math

import jax
import jax.numpy as jnp
from jax import lax
from jax.experimental import pallas as pl
from jax.experimental.pallas import tpu as pltpu
from jax.sharding import PartitionSpec as P

HD = 128
KERNEL = 7
HALO = 16
BLOCK = 256
DIGIT_ROWS = 16
DIGIT = 128
TILE = 512
LANES = 128
NEG = -2.0e38
OVERFLOW = 2.0**100
QUERY_SCALE = math.log2(math.e) / math.sqrt(HD)
VMEM_BYTES = 60 * 1024 * 1024
SCALE = 0.3


def taking(microseconds):
    return pl.CostEstimate(
        flops=int(microseconds * 1.1e9 * SCALE), bytes_accessed=1024, transcendentals=0
    )


def ring_shift(value, axis, by):
    size = lax.axis_size(axis)
    return lax.ppermute(value, axis, [(i, (i + by) % size) for i in range(size)])


def swap_bits(value, axis, bits):
    size = lax.axis_size(axis)
    return lax.ppermute(value, axis, [(i, i ^ bits) for i in range(size)])


def normed_rows(rows, gain):
    rows = rows.astype(jnp.float32)
    inverse = lax.rsqrt(jnp.mean(rows * rows, axis=-1, keepdims=True) + 1e-06)
    return (rows * inverse * gain).astype(jnp.bfloat16)


def project_kernel(n_heads, block, raw, heads, *refs):
    x_ref, halo_ref, gain_ref, w_ref, taps_ref, offs_ref, digits_ref = refs[:7]
    slabs = refs[7 : 7 + n_heads]
    rest = refs[7 + n_heads :]
    if raw:
        normed_ref, *rest = rest
    x_buf, halo_buf, w_buf, proj, out_buf, x_sems, w_sems, out_sems, n_sems = rest
    tiles = 3 * n_heads
    n_rows = x_ref.shape[0]
    n_blocks = n_rows // block

    def rows_copy(i):
        place = pl.ds(i * block, block)
        return pltpu.make_async_copy(x_ref.at[place, :], x_buf.at[place, :], x_sems.at[i])

    def weight_copy(tile):
        kind, slot = tile // n_heads, tile % n_heads
        start = pl.multiple_of(heads[slot] * HD, HD)
        return pltpu.make_async_copy(
            w_ref.at[kind, :, pl.ds(start, HD)],
            w_buf.at[:, pl.ds(tile * HD, HD)],
            w_sems.at[tile],
        )

    def out_copy(i, slot):
        place = pl.ds(i * block, block if i + 1 < n_blocks else block + DIGIT_ROWS)
        return pltpu.make_async_copy(
            out_buf.at[slot, :, place, :], slabs[slot].at[:, place, :], out_sems.at[i, slot]
        )

    rows_copy(0).start()
    for tile in range(tiles):
        weight_copy(tile).start()
    for i in range(1, n_blocks):
        rows_copy(i).start()

    def multiply(begin, first):
        width = 2 if raw else tiles
        for pair in range(0, tiles, width):
            some = range(pair, min(pair + width, tiles))
            if first:
                for tile in some:
                    weight_copy(tile).wait()
            w = w_buf[:, pair * HD : (some[-1] + 1) * HD]
            if first:
                before = jnp.dot(halo_buf[...], w, preferred_element_type=jnp.float32)
            here = x_buf[begin : begin + block, :]
            product = jnp.dot(here, w, preferred_element_type=jnp.float32)
            for tile in some:
                own = slice((tile - pair) * HD, (tile - pair + 1) * HD)
                if first:
                    proj[tile, :HALO, :] = before[:, own].astype(jnp.bfloat16).astype(jnp.float32)
                piece = product[:, own].astype(jnp.bfloat16).astype(jnp.float32)
                proj[tile, HALO + begin : HALO + begin + block, :] = piece

    def mix(i):
        begin = i * block
        offs = offs_ref[begin : begin + block, :]
        for tile in range(tiles):
            kind, slot = tile // n_heads, tile % n_heads
            start = pl.multiple_of(heads[slot] * HD, HD)
            taps = taps_ref[kind, :, pl.ds(start, HD)]
            total = taps[0:1, :] * proj[tile, HALO + begin : HALO + begin + block, :]
            for lag in range(1, KERNEL):
                at = HALO - lag + begin
                shifted = taps[lag : lag + 1, :] * proj[tile, at : at + block, :]
                total = total + jnp.where(offs >= lag, shifted, 0.0)
            if kind == 0:
                total = total * QUERY_SCALE
            out_buf[slot, kind, begin : begin + block, :] = total.astype(jnp.bfloat16)

    def normed_copy(i):
        place = pl.ds(i * block, block)
        return pltpu.make_async_copy(x_buf.at[place, :], normed_ref.at[place, :], n_sems.at[i])

    def rows_ready(i):
        rows_copy(i).wait()
        if raw:
            begin = i * block
            x_buf[begin : begin + block, :] = normed_rows(
                x_buf[begin : begin + block, :], gain_ref[...]
            )
            normed_copy(i).start()

    before_rows = normed_rows(halo_ref[...], gain_ref[...])
    halo_buf[...] = jnp.where(heads[n_heads] == 0, jnp.zeros_like(before_rows), before_rows)
    for slot in range(n_heads):
        for kind in range(3):
            out_buf[slot, kind, n_rows:, :] = digits_ref[...]
    rows_ready(0)
    multiply(0, True)
    for i in range(n_blocks):
        if i + 1 < n_blocks:
            rows_ready(i + 1)
            multiply((i + 1) * block, False)
        mix(i)
        for slot in range(n_heads):
            out_copy(i, slot).start()
    for i in range(n_blocks):
        for slot in range(n_heads):
            out_copy(i, slot).wait()
        if raw:
            normed_copy(i).wait()


def project(heads, rows, halo, gain, w, taps, offs, digits, block, raw):
    n_rows, width = rows.shape
    n_heads = heads.shape[0] - 1
    anywhere = pl.BlockSpec(memory_space=pl.ANY)
    vmem = pl.BlockSpec(memory_space=pltpu.VMEM)
    n_blocks = n_rows // block
    slab_rows = n_rows + DIGIT_ROWS
    out_shape = [jax.ShapeDtypeStruct((3, slab_rows, HD), jnp.bfloat16)] * n_heads
    if raw:
        out_shape.append(jax.ShapeDtypeStruct(rows.shape, jnp.bfloat16))
    return pl.pallas_call(
        functools.partial(project_kernel, n_heads, block, raw),
        out_shape=out_shape,
        grid_spec=pltpu.PrefetchScalarGridSpec(
            num_scalar_prefetch=1,
            grid=(),
            in_specs=[anywhere, vmem, vmem, anywhere, vmem, vmem, vmem],
            out_specs=[anywhere] * len(out_shape),
            scratch_shapes=[
                pltpu.VMEM((n_rows, width), jnp.bfloat16),
                pltpu.VMEM((HALO, width), jnp.bfloat16),
                pltpu.VMEM((width, 3 * n_heads * HD), jnp.bfloat16),
                pltpu.VMEM((3 * n_heads, HALO + n_rows, HD), jnp.float32),
                pltpu.VMEM((n_heads, 3, slab_rows, HD), jnp.bfloat16),
                pltpu.SemaphoreType.DMA((n_blocks,)),
                pltpu.SemaphoreType.DMA((3 * n_heads,)),
                pltpu.SemaphoreType.DMA((n_blocks, n_heads)),
                pltpu.SemaphoreType.DMA((n_blocks,)),
            ],
        ),
        compiler_params=pltpu.CompilerParams(vmem_limit_bytes=VMEM_BYTES),
        cost_estimate=taking(6 + 6 * n_heads),
    )(heads, rows, halo, gain, w, taps, offs, digits)


def attend_kernel(
    kv_sources, n_all, slabs, paired, rows_block, row0, chunk, tile_rows, where, *refs
):
    n_slabs = len(slabs)
    n_pieces = 1 + max(max(k[0], v[0]) for k, v in kv_sources)
    pieces = refs[:n_pieces]
    outs = refs[n_pieces : n_pieces + n_slabs]
    rest = refs[n_pieces + n_slabs :]
    k_buf, v_buf, q_buf, digits, first_ref, out_buf, top, total, acc, kv_sems, q_sems, out_sems = rest
    group = len(kv_sources) // n_all
    hi, lo = where[0], where[1]

    def slot_of(block):
        within = block % group
        if paired:
            within = jnp.bitwise_xor(within, lo)
        return jnp.bitwise_xor(block // group, hi) * group + within

    q_copies = []
    for slab in range(n_slabs):
        q_copies.append(
            pltpu.make_async_copy(
                pieces[slabs[slab]].at[0, pl.ds(row0, chunk), :],
                q_buf.at[pl.ds(slab * chunk, chunk), :],
                q_sems.at[0, slab],
            )
        )
        q_copies.append(
            pltpu.make_async_copy(
                pieces[slabs[slab]].at[0, pl.ds(rows_block, DIGIT_ROWS), :],
                digits.at[slab],
                q_sems.at[1, slab],
            )
        )
    for copy in q_copies:
        copy.start()
    for slot, (k_at, v_at) in enumerate(kv_sources):
        place = pl.ds(slot * rows_block, rows_block)
        for at, buf, side in ((k_at, k_buf, 0), (v_at, v_buf, 1)):
            source = pieces[at[0]].at[at[1], pl.ds(0, rows_block), :]
            pltpu.make_async_copy(source, buf.at[place, :], kv_sems.at[side, slot]).start()

    def wait_for_block(block, c):
        slot = slot_of(block)
        place = pl.ds(pl.multiple_of(slot * rows_block, rows_block), rows_block)
        for at, buf, side in ((kv_sources[0][0], k_buf, 0), (kv_sources[0][1], v_buf, 1)):
            source = pieces[at[0]].at[at[1], pl.ds(0, rows_block), :]
            pltpu.make_async_copy(source, buf.at[place, :], kv_sems.at[side, slot]).wait()
        return c

    for copy in q_copies:
        copy.wait()

    shape = (LANES, LANES)
    rows = lax.broadcasted_iota(jnp.int32, shape, 0)
    same = rows == lax.broadcasted_iota(jnp.int32, shape, 1)
    ones = jnp.ones(shape, jnp.bfloat16)
    for slab in range(n_slabs):
        block = jnp.bitwise_xor(hi, slabs[slab]) * group + lo
        both = digits[slab].astype(jnp.float32)
        for part in range(chunk // LANES):
            line = row0 // LANES + part

            def down(row):
                across = jnp.where(same, jnp.broadcast_to(both[row : row + 1, :], shape), 0.0)
                return jnp.dot(
                    across.astype(jnp.bfloat16), ones, preferred_element_type=jnp.float32
                )

            offset = down(line) * DIGIT + down(DIGIT_ROWS // 2 + line)
            begin = block * rows_block + row0 + part * LANES
            at = slab * chunk + part * LANES
            first_ref[at : at + LANES, :] = begin + rows - offset.astype(jnp.int32)

    tiles = chunk // tile_rows
    wide = tile_rows // LANES
    pair = rows_block // tile_rows

    def spread(column, count=1):
        return jnp.concatenate([column] * (wide * count), axis=1)

    def one_query_tile(index, begin):
        at = pl.multiple_of(index * tile_rows, tile_rows)
        first_low = jnp.min(first_ref[pl.ds(at, 8), :])
        first_high = jnp.max(first_ref[pl.ds(at + tile_rows - 8, 8), :])
        q = q_buf[pl.ds(at, tile_rows), :]
        diagonal = begin // tile_rows

        def key_rows(tile, count=1):
            key_begin = tile * tile_rows
            slot = slot_of(key_begin // rows_block)
            row = slot * rows_block + key_begin % rows_block
            return pl.ds(pl.multiple_of(row, tile_rows), count * tile_rows)

        def scores_of(tile, lower, upper, count=1):
            shape = (tile_rows, count * tile_rows)
            scores = lax.dot_general(
                q,
                k_buf[key_rows(tile, count), :],
                (((1,), (1,)), ((), ())),
                preferred_element_type=jnp.float32,
            )
            if lower or upper:
                lane = lax.broadcasted_iota(jnp.int32, shape, 1)
            if lower:
                first = first_ref[pl.ds(at, tile_rows), :] - tile * tile_rows
                scores = jnp.where(lane >= spread(first), scores, NEG)
            if upper:
                row = lax.broadcasted_iota(jnp.int32, shape, 0)
                scores = jnp.where(lane <= row, scores, NEG)
            return scores

        def weighed(tile, weights, count=1):
            part = weights[:, :LANES]
            for piece in range(1, wide * count):
                part = part + weights[:, piece * LANES : (piece + 1) * LANES]
            product = jnp.dot(
                weights.astype(jnp.bfloat16),
                v_buf[key_rows(tile, count), :],
                preferred_element_type=jnp.float32,
            )
            return product, part

        def fixed_top(tile, lower, count=1):
            scores = scores_of(tile, lower, False, count)
            weights = jnp.exp2(scores - spread(top[...], count))
            product, part = weighed(tile, weights, count)
            acc[...] += product
            total[...] += part

        def masked_tile(tile, c):
            fixed_top(tile, True)
            return c

        def open_tile(tile, c):
            fixed_top(tile, False)
            return c

        def open_block(block, c):
            fixed_top(block * pair, False, pair)
            return c

        key_low = first_low // tile_rows
        open_low = jnp.minimum((first_high + tile_rows - 1) // tile_rows, diagonal)
        scores = scores_of(diagonal, True, True)
        top[...] = jnp.broadcast_to(jnp.max(scores, axis=1, keepdims=True), top.shape)
        acc[...], total[...] = weighed(diagonal, jnp.exp2(scores - spread(top[...])))
        lax.fori_loop(key_low, open_low, masked_tile, 0)
        block_end = diagonal // pair
        block_low = (open_low + pair - 1) // pair
        lax.fori_loop(open_low, jnp.minimum(block_low * pair, diagonal), open_tile, 0)
        lax.fori_loop(block_low, block_end, open_block, 0)
        lax.fori_loop(jnp.maximum(block_end * pair, jnp.minimum(block_low * pair, diagonal)), diagonal, open_tile, 0)

        @pl.when(jnp.logical_not(jnp.max(total[...]) < OVERFLOW))
        def _():
            top[...] = jnp.full(top.shape, NEG, jnp.float32)
            total[...] = jnp.zeros(total.shape, jnp.float32)
            acc[...] = jnp.zeros(acc.shape, jnp.float32)

            def running(tile, upper):
                scores = scores_of(tile, True, upper)
                old = top[...]
                new = jnp.maximum(old, jnp.max(scores, axis=1, keepdims=True))
                factor = jnp.exp2(old - new)
                product, part = weighed(tile, jnp.exp2(scores - spread(new)))
                acc[...] = acc[...] * factor + product
                total[...] = total[...] * factor + part
                top[...] = new

            def running_tile(tile, c):
                running(tile, False)
                return c

            lax.fori_loop(key_low, diagonal, running_tile, 0)
            running(diagonal, True)

        summed = jnp.sum(total[...], axis=1, keepdims=True)
        out_buf[pl.ds(at, tile_rows), :] = (acc[...] / summed).astype(jnp.bfloat16)

    def one_slab(order, waited):
        slab = jnp.bitwise_xor(hi, order)
        block = order * group + lo
        index, here = 0, slab == slabs[0]
        for number in range(1, n_slabs):
            index = jnp.where(slab == slabs[number], number, index)
            here = here | (slab == slabs[number])
        wanted = jnp.where(here, block + 1, waited)
        lax.fori_loop(waited, wanted, wait_for_block, 0)

        def one_tile(part, c):
            one_query_tile(index * tiles + part, block * rows_block + row0 + part * tile_rows)
            return c

        lax.fori_loop(0, jnp.where(here, tiles, 0), one_tile, 0)
        return wanted

    waited = lax.fori_loop(0, n_all, one_slab, 0)
    lax.fori_loop(waited, len(kv_sources), wait_for_block, 0)
    out_copies = [
        pltpu.make_async_copy(
            out_buf.at[pl.ds(slab * chunk, chunk), :], outs[slab], out_sems.at[slab]
        )
        for slab in range(n_slabs)
    ]
    for copy in out_copies:
        copy.start()
    for copy in out_copies:
        copy.wait()


def attend(pieces, kv_sources, where, slabs, paired, rows_block, row0, chunk):
    n_slots = len(kv_sources)
    n_slabs = len(slabs)
    n_all = len(pieces) // 2
    tile_rows = min(TILE, chunk)
    anywhere = pl.BlockSpec(memory_space=pl.ANY)
    return pl.pallas_call(
        functools.partial(
            attend_kernel, kv_sources, n_all, slabs, paired, rows_block, row0, chunk, tile_rows
        ),
        out_shape=[jax.ShapeDtypeStruct((chunk, HD), jnp.bfloat16)] * n_slabs,
        grid_spec=pltpu.PrefetchScalarGridSpec(
            num_scalar_prefetch=1,
            grid=(),
            in_specs=[anywhere] * len(pieces),
            out_specs=[anywhere] * n_slabs,
            scratch_shapes=[
                pltpu.VMEM((n_slots * rows_block, HD), jnp.bfloat16),
                pltpu.VMEM((n_slots * rows_block, HD), jnp.bfloat16),
                pltpu.VMEM((n_slabs * chunk, HD), jnp.bfloat16),
                pltpu.VMEM((n_slabs, DIGIT_ROWS, LANES), jnp.bfloat16),
                pltpu.VMEM((n_slabs * chunk, LANES), jnp.int32),
                pltpu.VMEM((n_slabs * chunk, HD), jnp.bfloat16),
                pltpu.VMEM((tile_rows, LANES), jnp.float32),
                pltpu.VMEM((tile_rows, LANES), jnp.float32),
                pltpu.VMEM((tile_rows, HD), jnp.float32),
                pltpu.SemaphoreType.DMA((2, n_slots)),
                pltpu.SemaphoreType.DMA((2, n_slabs)),
                pltpu.SemaphoreType.DMA((n_slabs,)),
            ],
        ),
        compiler_params=pltpu.CompilerParams(vmem_limit_bytes=VMEM_BYTES),
        cost_estimate=taking(2 + 4 * n_slabs),
    )(where, *pieces)


def out_kernel(parts, n_w, row0, has_sum, last, where, *refs):
    n_atts = len(parts)
    atts = refs[:n_atts]
    w_own, *rest = refs[n_atts:]
    w_parts, (tok_ref, *rest) = rest[:n_w], rest[n_w:]
    if has_sum:
        sum_ref, *rest = rest
    if last and row0:
        rest = rest[1:]
    out_ref, a_buf, w_buf, t_buf, o_buf, a_sems, w_sems, x_sems = rest
    hi, plane = where[0], where[2]
    rows, cols = o_buf.shape
    copies, waits = [], []
    col0 = pl.multiple_of(plane * cols, cols)
    at = 0
    for number, (step, slabs) in enumerate(parts):
        for place, slab in enumerate(slabs):
            copies.append(
                pltpu.make_async_copy(
                    atts[number].at[place], a_buf.at[:, pl.ds(at * HD, HD)], a_sems.at[at]
                )
            )
            head = jnp.bitwise_xor(hi, slab)
            into = w_buf.at[pl.ds(at * HD, HD), :]
            if step == 0:
                row = pl.multiple_of(head * HD, HD)
                source = w_own.at[pl.ds(row, HD), pl.ds(col0, cols)]
                copies.append(pltpu.make_async_copy(source, into, w_sems.at[at]))
            elif n_w == 1:
                row = pl.multiple_of(head * HD, HD)
                source = w_parts[0].at[step - 1, pl.ds(row, HD), :]
                copies.append(pltpu.make_async_copy(source, into, w_sems.at[at]))
            else:
                side = cols // 2
                for bit in range(2):
                    which = jnp.bitwise_xor(head, 2 * (hi >> bit & 1) + where[1])
                    target = w_buf.at[pl.ds(at * HD, HD), pl.ds(bit * side, side)]
                    for turn in range(n_w // 2):
                        source = w_parts[bit * (n_w // 2) + turn].at[step - 1]

                        def fetch(source=source, target=target, at=at):
                            pltpu.make_async_copy(source, target, w_sems.at[at]).start()

                        pl.when(which == turn)(fetch)
                waits.append(pltpu.make_async_copy(into, into, w_sems.at[at]))
            at += 1
    if has_sum:
        copies.append(pltpu.make_async_copy(sum_ref, t_buf, x_sems.at[0]))
    else:
        tok = tok_ref.at[pl.ds(row0, rows), pl.ds(col0, cols)]
        copies.append(pltpu.make_async_copy(tok, t_buf, x_sems.at[0]))
    for copy in copies:
        copy.start()
    for copy in copies + waits:
        copy.wait()
    product = jnp.dot(a_buf[...], w_buf[...], preferred_element_type=jnp.float32)
    o_buf[...] = (t_buf[...].astype(jnp.float32) + product).astype(o_buf.dtype)
    target = out_ref.at[pl.ds(row0, rows), :] if last else out_ref
    done = pltpu.make_async_copy(o_buf, target, x_sems.at[1])
    done.start()
    done.wait()


def project_out(where, parts, atts, w_own, w_parts, n_cols, tokens, row0, total, so_far, last):
    rows = atts[0].shape[1]
    n_rows, cols = tokens.shape[0], n_cols
    depth = sum(att.shape[0] for att in atts) * HD
    anywhere = pl.BlockSpec(memory_space=pl.ANY)
    operands = [*atts, w_own, *w_parts, tokens]
    has_sum = total is not None
    if has_sum:
        operands.append(total)
    aliases = {}
    if last and row0:
        aliases = {len(operands) + 1: 0}
        operands.append(so_far)
    kind = jnp.bfloat16 if last else jnp.float32
    return pl.pallas_call(
        functools.partial(out_kernel, parts, len(w_parts), row0, has_sum, last),
        out_shape=jax.ShapeDtypeStruct((n_rows if last else rows, cols), kind),
        grid_spec=pltpu.PrefetchScalarGridSpec(
            num_scalar_prefetch=1,
            grid=(),
            in_specs=[anywhere] * len(operands),
            out_specs=anywhere,
            scratch_shapes=[
                pltpu.VMEM((rows, depth), jnp.bfloat16),
                pltpu.VMEM((depth, cols), jnp.bfloat16),
                pltpu.VMEM((rows, cols), jnp.float32 if has_sum else jnp.bfloat16),
                pltpu.VMEM((rows, cols), kind),
                pltpu.SemaphoreType.DMA((depth // HD,)),
                pltpu.SemaphoreType.DMA((depth // HD,)),
                pltpu.SemaphoreType.DMA((2,)),
            ],
        ),
        input_output_aliases=aliases,
        compiler_params=pltpu.CompilerParams(vmem_limit_bytes=VMEM_BYTES),
        cost_estimate=taking(6),
    )(where, *operands)


def after(value, *others):
    return lax.optimization_barrier((value, *others))[0]


def shards(tokens, norm_gain, w_qkv, conv_filter, w_out, contig_offsets):
    n_rows, width = tokens.shape
    n_heads = w_qkv.shape[2] // HD
    n_ctx, n_planes = lax.axis_size("ctx"), lax.axis_size("mp")
    ctx, plane = lax.axis_index("ctx"), lax.axis_index("mp")
    group = n_ctx // n_heads
    assert group * n_heads == n_ctx and n_heads & (n_heads - 1) == 0
    hi, lo = ctx // group, ctx % group
    paired = group == 2 and n_heads % 2 == 0
    cols = width // n_planes
    where = jnp.stack([hi, lo, plane]).astype(jnp.int32)

    halo = ring_shift(tokens[n_rows - HALO :], "ctx", 1)
    w = w_qkv.transpose(1, 0, 2)
    taps = conv_filter.transpose(1, 0, 2)
    offs = jnp.broadcast_to(contig_offsets[:, None], (n_rows, LANES))
    lines = contig_offsets.reshape(n_rows // LANES, LANES)
    assert lines.shape[0] * 2 == DIGIT_ROWS
    digits = jnp.concatenate([lines // DIGIT, lines % DIGIT], axis=0).astype(jnp.bfloat16)
    gain = norm_gain[None, :]

    def run_project(batch, rows, raw):
        heads = jnp.stack([jnp.bitwise_xor(hi, k) for k in batch] + [ctx]).astype(jnp.int32)
        block = BLOCK if raw else n_rows
        return project(heads, rows, halo, gain, w, taps, offs, digits, block, raw)

    def send(slab, k):
        return swap_bits(slab, "ctx", k * group) if k else slab

    def w_piece(step, tied):
        half = n_heads // 2 * HD
        col0 = (plane + step) % n_planes * cols
        piece = lax.dynamic_slice(after(w_out, *tied), (lo * half, col0), (half, cols))
        return ring_shift(piece, "mp", step)

    own = [None] * n_heads
    if paired:
        far = n_heads - 1
        *slabs, normed = run_project([far], tokens, True)
        own[far] = send(slabs[0], far)
        side = cols // 2
        w_got = {}

        def bring(step, tied):
            begin = (plane + step) % n_planes * cols
            source = after(w_out, tied)
            both = [
                lax.dynamic_slice(
                    source, ((2 * (hi >> bit & 1) + lo) * HD, begin + bit * side), (HD, side)
                )
                for bit in range(2)
            ]
            w_got[step] = ring_shift(jnp.stack(both), "mp", step)

        for step in range(1, n_planes):
            bring(step, slabs[0])
        near = list(range(1, far))
        slabs = run_project(near, normed, False)
        slabs, own[far], w_got = lax.optimization_barrier((slabs, own[far], w_got))
        for k, slab in zip(near, slabs):
            own[k] = send(slab, k)
        own[0] = run_project([0], after(normed, slabs[0]), False)[0]
        w_got = [w_got[step] for step in range(1, n_planes)]
    else:
        order = list(range(n_heads))
        *slabs, _ = run_project(order, tokens, True)
        own = [send(slab, k) for k, slab in zip(order, slabs)]
        by_plane = w_out.reshape(n_heads * HD, n_planes, cols).transpose(1, 0, 2)
        got = lax.all_to_all(by_plane, "mp", split_axis=0, concat_axis=0, tiled=True)
        w_parts = [got[(plane - jnp.arange(1, n_planes)) % n_planes]]

    pieces = list(own)
    kv_sources = []
    if paired:
        pieces += [
            swap_bits(after(own[k], own[0]) if k else own[0], "ctx", 1) for k in range(n_heads)
        ]
        for k in range(n_heads):
            kv_sources += [((k, 1), (k, 2)), ((n_heads + k, 1), (n_heads + k, 2))]
    else:
        groups = [[a * group + b for b in range(group)] for a in range(n_heads)]
        for k, slab in enumerate(own):
            pieces.append(
                lax.all_gather(slab[1:, :n_rows], "ctx", axis=0, tiled=True, axis_index_groups=groups)
            )
            kv_sources += [((n_heads + k, 2 * b), (n_heads + k, 2 * b + 1)) for b in range(group)]
    n_chunks = 2
    chunk = n_rows // n_chunks

    everyone = tuple(range(n_heads))

    def run_attend(part, tied, slabs=everyone):
        at = after(where, *tied)
        return attend(pieces, kv_sources, at, slabs, paired, n_rows, part * chunk, chunk)

    def bring_home(outs, slabs=everyone):
        return jnp.stack([send(out, k) for k, out in zip(slabs, outs)])

    def run_out(part, some, total, so_far, last):
        return project_out(
            where, [p for p, _ in some], [a for _, a in some], w_out, w_parts,
            cols, tokens, part * chunk, total, so_far, last,
        )

    result = None
    if n_planes > 4 or not paired:
        for part in range(n_chunks):
            att = bring_home(run_attend(part, ()))
            gathered = lax.all_gather(att, "mp", axis=0)
            some = [((d, everyone), gathered[(plane - d) % n_planes]) for d in range(n_planes)]
            result = run_out(part, some, None, result, True)
        return result

    half = n_heads // 2
    w_near = jnp.stack(w_got, axis=1)
    w_next = swap_bits(w_near, "ctx", 1)
    w_parts = []
    for bit in range(2):
        mine = [w_near[bit], w_next[bit]]
        w_parts += mine + [swap_bits(part, "ctx", group << bit) for part in mine]
    outs = run_attend(0, ())
    outs = [after(out, w_parts[2], w_parts[3], w_parts[6], w_parts[7]) for out in outs]
    early = [bring_home(outs)]
    turns = [(k, n_heads - 1 - k) for k in range(half)]
    held = []
    tied = (early[0],)
    for pair in turns:
        early.append(ring_shift(after(early[-1], *tied), "mp", 1))
        outs = run_attend(1, tied, pair)
        tied = (outs[0], early[-1])
        if held:
            outs = [after(out, early[-1], held[-1][-1]) for out in outs]
        mine = bring_home(outs, pair)
        held.append([mine, ring_shift(mine, "mp", 1)])
        tied = (*tied, mine)
    while len(early) < n_planes:
        early.append(ring_shift(after(early[-1], *tied[:2]), "mp", 1))
    result = run_out(0, list(zip([(d, everyone) for d in range(n_planes)], early)), None, None, True)
    for step in range(2, n_planes):
        for ring in held:
            ahead = ring[-1]
            if step == n_planes - 1:
                ahead = after(ahead, result)
            ring.append(ring_shift(ahead, "mp", 1))
    late = [((d, pair), ring[d]) for d in range(n_planes) for pair, ring in zip(turns, held)]
    total = run_out(1, late[: -len(turns)], None, None, False)
    return run_out(1, late[-len(turns) :], total, result, True)


def solution(mesh):
    placed = (
        P("ctx", None),
        P(),
        P(None, None, "mp"),
        P(None, None, "mp"),
        P("mp", None),
        P("ctx"),
    )
    return jax.shard_map(
        shards, mesh=mesh, in_specs=placed, out_specs=P("ctx", "mp"), check_vma=False
    )
```

```python
import functools
import math

import jax
import jax.numpy as jnp
from jax import lax
from jax.experimental import pallas as pl
from jax.experimental.pallas import tpu as pltpu
from jax.sharding import PartitionSpec as P

HD = 128
KERNEL = 7
HALO = 16
BLOCK = 256
DIGIT_ROWS = 16
DIGIT = 128
TILE = 512
LANES = 128
NEG = -2.0e38
OVERFLOW = 2.0**100
QUERY_SCALE = math.log2(math.e) / math.sqrt(HD)
VMEM_BYTES = 60 * 1024 * 1024
SCALE = 0.3


def taking(microseconds):
    return pl.CostEstimate(
        flops=int(microseconds * 1.1e9 * SCALE), bytes_accessed=1024, transcendentals=0
    )


def ring_shift(value, axis, by):
    size = lax.axis_size(axis)
    return lax.ppermute(value, axis, [(i, (i + by) % size) for i in range(size)])


def swap_bits(value, axis, bits):
    size = lax.axis_size(axis)
    return lax.ppermute(value, axis, [(i, i ^ bits) for i in range(size)])


def normed_rows(rows, gain):
    rows = rows.astype(jnp.float32)
    inverse = lax.rsqrt(jnp.mean(rows * rows, axis=-1, keepdims=True) + 1e-06)
    return (rows * inverse * gain).astype(jnp.bfloat16)


def project_kernel(n_heads, block, raw, heads, *refs):
    x_ref, halo_ref, gain_ref, w_ref, taps_ref, offs_ref, digits_ref = refs[:7]
    slabs = refs[7 : 7 + n_heads]
    rest = refs[7 + n_heads :]
    if raw:
        normed_ref, *rest = rest
    x_buf, halo_buf, w_buf, proj, out_buf, x_sems, w_sems, out_sems, n_sems = rest
    tiles = 3 * n_heads
    n_rows = x_ref.shape[0]
    n_blocks = n_rows // block

    def rows_copy(i):
        place = pl.ds(i * block, block)
        return pltpu.make_async_copy(x_ref.at[place, :], x_buf.at[place, :], x_sems.at[i])

    def weight_copy(tile):
        kind, slot = tile // n_heads, tile % n_heads
        start = pl.multiple_of(heads[slot] * HD, HD)
        return pltpu.make_async_copy(
            w_ref.at[kind, :, pl.ds(start, HD)],
            w_buf.at[:, pl.ds(tile * HD, HD)],
            w_sems.at[tile],
        )

    def out_copy(i, slot):
        place = pl.ds(i * block, block if i + 1 < n_blocks else block + DIGIT_ROWS)
        return pltpu.make_async_copy(
            out_buf.at[slot, :, place, :], slabs[slot].at[:, place, :], out_sems.at[i, slot]
        )

    rows_copy(0).start()
    for tile in range(tiles):
        weight_copy(tile).start()
    for i in range(1, n_blocks):
        rows_copy(i).start()

    def multiply(begin, first):
        width = 2 if raw else tiles
        for pair in range(0, tiles, width):
            some = range(pair, min(pair + width, tiles))
            if first:
                for tile in some:
                    weight_copy(tile).wait()
            w = w_buf[:, pair * HD : (some[-1] + 1) * HD]
            if first:
                before = jnp.dot(halo_buf[...], w, preferred_element_type=jnp.float32)
            here = x_buf[begin : begin + block, :]
            product = jnp.dot(here, w, preferred_element_type=jnp.float32)
            for tile in some:
                own = slice((tile - pair) * HD, (tile - pair + 1) * HD)
                if first:
                    proj[tile, :HALO, :] = before[:, own].astype(jnp.bfloat16).astype(jnp.float32)
                piece = product[:, own].astype(jnp.bfloat16).astype(jnp.float32)
                proj[tile, HALO + begin : HALO + begin + block, :] = piece

    def mix(i):
        begin = i * block
        offs = offs_ref[begin : begin + block, :]
        for tile in range(tiles):
            kind, slot = tile // n_heads, tile % n_heads
            start = pl.multiple_of(heads[slot] * HD, HD)
            taps = taps_ref[kind, :, pl.ds(start, HD)]
            total = taps[0:1, :] * proj[tile, HALO + begin : HALO + begin + block, :]
            for lag in range(1, KERNEL):
                at = HALO - lag + begin
                shifted = taps[lag : lag + 1, :] * proj[tile, at : at + block, :]
                total = total + jnp.where(offs >= lag, shifted, 0.0)
            if kind == 0:
                total = total * QUERY_SCALE
            out_buf[slot, kind, begin : begin + block, :] = total.astype(jnp.bfloat16)

    def normed_copy(i):
        place = pl.ds(i * block, block)
        return pltpu.make_async_copy(x_buf.at[place, :], normed_ref.at[place, :], n_sems.at[i])

    def rows_ready(i):
        rows_copy(i).wait()
        if raw:
            begin = i * block
            x_buf[begin : begin + block, :] = normed_rows(
                x_buf[begin : begin + block, :], gain_ref[...]
            )
            normed_copy(i).start()

    before_rows = normed_rows(halo_ref[...], gain_ref[...])
    halo_buf[...] = jnp.where(heads[n_heads] == 0, jnp.zeros_like(before_rows), before_rows)
    for slot in range(n_heads):
        for kind in range(3):
            out_buf[slot, kind, n_rows:, :] = digits_ref[...]
    rows_ready(0)
    multiply(0, True)
    for i in range(n_blocks):
        if i + 1 < n_blocks:
            rows_ready(i + 1)
            multiply((i + 1) * block, False)
        mix(i)
        for slot in range(n_heads):
            out_copy(i, slot).start()
    for i in range(n_blocks):
        for slot in range(n_heads):
            out_copy(i, slot).wait()
        if raw:
            normed_copy(i).wait()


def project(heads, rows, halo, gain, w, taps, offs, digits, block, raw):
    n_rows, width = rows.shape
    n_heads = heads.shape[0] - 1
    anywhere = pl.BlockSpec(memory_space=pl.ANY)
    vmem = pl.BlockSpec(memory_space=pltpu.VMEM)
    n_blocks = n_rows // block
    slab_rows = n_rows + DIGIT_ROWS
    out_shape = [jax.ShapeDtypeStruct((3, slab_rows, HD), jnp.bfloat16)] * n_heads
    if raw:
        out_shape.append(jax.ShapeDtypeStruct(rows.shape, jnp.bfloat16))
    return pl.pallas_call(
        functools.partial(project_kernel, n_heads, block, raw),
        out_shape=out_shape,
        grid_spec=pltpu.PrefetchScalarGridSpec(
            num_scalar_prefetch=1,
            grid=(),
            in_specs=[anywhere, vmem, vmem, anywhere, vmem, vmem, vmem],
            out_specs=[anywhere] * len(out_shape),
            scratch_shapes=[
                pltpu.VMEM((n_rows, width), jnp.bfloat16),
                pltpu.VMEM((HALO, width), jnp.bfloat16),
                pltpu.VMEM((width, 3 * n_heads * HD), jnp.bfloat16),
                pltpu.VMEM((3 * n_heads, HALO + n_rows, HD), jnp.float32),
                pltpu.VMEM((n_heads, 3, slab_rows, HD), jnp.bfloat16),
                pltpu.SemaphoreType.DMA((n_blocks,)),
                pltpu.SemaphoreType.DMA((3 * n_heads,)),
                pltpu.SemaphoreType.DMA((n_blocks, n_heads)),
                pltpu.SemaphoreType.DMA((n_blocks,)),
            ],
        ),
        compiler_params=pltpu.CompilerParams(vmem_limit_bytes=VMEM_BYTES),
        cost_estimate=taking(6 + 6 * n_heads),
    )(heads, rows, halo, gain, w, taps, offs, digits)


def attend_kernel(
    kv_sources, n_all, slabs, paired, rows_block, row0, chunk, tile_rows, where, *refs
):
    n_slabs = len(slabs)
    n_pieces = 1 + max(max(k[0], v[0]) for k, v in kv_sources)
    pieces = refs[:n_pieces]
    outs = refs[n_pieces : n_pieces + n_slabs]
    rest = refs[n_pieces + n_slabs :]
    k_buf, v_buf, q_buf, digits, first_ref, out_buf, top, total, acc, kv_sems, q_sems, out_sems = rest
    group = len(kv_sources) // n_all
    hi, lo = where[0], where[1]

    def slot_of(block):
        within = block % group
        if paired:
            within = jnp.bitwise_xor(within, lo)
        return jnp.bitwise_xor(block // group, hi) * group + within

    q_copies = []
    for slab in range(n_slabs):
        q_copies.append(
            pltpu.make_async_copy(
                pieces[slabs[slab]].at[0, pl.ds(row0, chunk), :],
                q_buf.at[pl.ds(slab * chunk, chunk), :],
                q_sems.at[0, slab],
            )
        )
        q_copies.append(
            pltpu.make_async_copy(
                pieces[slabs[slab]].at[0, pl.ds(rows_block, DIGIT_ROWS), :],
                digits.at[slab],
                q_sems.at[1, slab],
            )
        )
    for copy in q_copies:
        copy.start()
    for slot, (k_at, v_at) in enumerate(kv_sources):
        place = pl.ds(slot * rows_block, rows_block)
        for at, buf, side in ((k_at, k_buf, 0), (v_at, v_buf, 1)):
            source = pieces[at[0]].at[at[1], pl.ds(0, rows_block), :]
            pltpu.make_async_copy(source, buf.at[place, :], kv_sems.at[side, slot]).start()

    def wait_for_block(block, c):
        slot = slot_of(block)
        place = pl.ds(pl.multiple_of(slot * rows_block, rows_block), rows_block)
        for at, buf, side in ((kv_sources[0][0], k_buf, 0), (kv_sources[0][1], v_buf, 1)):
            source = pieces[at[0]].at[at[1], pl.ds(0, rows_block), :]
            pltpu.make_async_copy(source, buf.at[place, :], kv_sems.at[side, slot]).wait()
        return c

    for copy in q_copies:
        copy.wait()

    shape = (LANES, LANES)
    rows = lax.broadcasted_iota(jnp.int32, shape, 0)
    same = rows == lax.broadcasted_iota(jnp.int32, shape, 1)
    ones = jnp.ones(shape, jnp.bfloat16)
    for slab in range(n_slabs):
        block = jnp.bitwise_xor(hi, slabs[slab]) * group + lo
        both = digits[slab].astype(jnp.float32)
        for part in range(chunk // LANES):
            line = row0 // LANES + part

            def down(row):
                across = jnp.where(same, jnp.broadcast_to(both[row : row + 1, :], shape), 0.0)
                return jnp.dot(
                    across.astype(jnp.bfloat16), ones, preferred_element_type=jnp.float32
                )

            offset = down(line) * DIGIT + down(DIGIT_ROWS // 2 + line)
            begin = block * rows_block + row0 + part * LANES
            at = slab * chunk + part * LANES
            first_ref[at : at + LANES, :] = begin + rows - offset.astype(jnp.int32)

    tiles = chunk // tile_rows
    wide = tile_rows // LANES
    pair = rows_block // tile_rows

    def spread(column, count=1):
        return jnp.concatenate([column] * (wide * count), axis=1)

    def one_query_tile(index, begin):
        at = pl.multiple_of(index * tile_rows, tile_rows)
        first_low = jnp.min(first_ref[pl.ds(at, 8), :])
        first_high = jnp.max(first_ref[pl.ds(at + tile_rows - 8, 8), :])
        q = q_buf[pl.ds(at, tile_rows), :]
        diagonal = begin // tile_rows

        def key_rows(tile, count=1):
            key_begin = tile * tile_rows
            slot = slot_of(key_begin // rows_block)
            row = slot * rows_block + key_begin % rows_block
            return pl.ds(pl.multiple_of(row, tile_rows), count * tile_rows)

        def scores_of(tile, lower, upper, count=1):
            shape = (tile_rows, count * tile_rows)
            scores = lax.dot_general(
                q,
                k_buf[key_rows(tile, count), :],
                (((1,), (1,)), ((), ())),
                preferred_element_type=jnp.float32,
            )
            if lower or upper:
                lane = lax.broadcasted_iota(jnp.int32, shape, 1)
            if lower:
                first = first_ref[pl.ds(at, tile_rows), :] - tile * tile_rows
                scores = jnp.where(lane >= spread(first), scores, NEG)
            if upper:
                row = lax.broadcasted_iota(jnp.int32, shape, 0)
                scores = jnp.where(lane <= row, scores, NEG)
            return scores

        def weighed(tile, weights, count=1):
            part = weights[:, :LANES]
            for piece in range(1, wide * count):
                part = part + weights[:, piece * LANES : (piece + 1) * LANES]
            product = jnp.dot(
                weights.astype(jnp.bfloat16),
                v_buf[key_rows(tile, count), :],
                preferred_element_type=jnp.float32,
            )
            return product, part

        def fixed_top(tile, lower, count=1):
            scores = scores_of(tile, lower, False, count)
            weights = jnp.exp2(scores - spread(top[...], count))
            product, part = weighed(tile, weights, count)
            acc[...] += product
            total[...] += part

        def masked_tile(tile, c):
            fixed_top(tile, True)
            return c

        def open_tile(tile, c):
            fixed_top(tile, False)
            return c

        def open_block(block, c):
            fixed_top(block * pair, False, pair)
            return c

        key_low = first_low // tile_rows
        open_low = jnp.minimum((first_high + tile_rows - 1) // tile_rows, diagonal)
        scores = scores_of(diagonal, True, True)
        top[...] = jnp.broadcast_to(jnp.max(scores, axis=1, keepdims=True), top.shape)
        acc[...], total[...] = weighed(diagonal, jnp.exp2(scores - spread(top[...])))
        lax.fori_loop(key_low, open_low, masked_tile, 0)
        block_end = diagonal // pair
        block_low = (open_low + pair - 1) // pair
        lax.fori_loop(open_low, jnp.minimum(block_low * pair, diagonal), open_tile, 0)
        lax.fori_loop(block_low, block_end, open_block, 0)
        lax.fori_loop(jnp.maximum(block_end * pair, jnp.minimum(block_low * pair, diagonal)), diagonal, open_tile, 0)

        @pl.when(jnp.logical_not(jnp.max(total[...]) < OVERFLOW))
        def _():
            top[...] = jnp.full(top.shape, NEG, jnp.float32)
            total[...] = jnp.zeros(total.shape, jnp.float32)
            acc[...] = jnp.zeros(acc.shape, jnp.float32)

            def running(tile, upper):
                scores = scores_of(tile, True, upper)
                old = top[...]
                new = jnp.maximum(old, jnp.max(scores, axis=1, keepdims=True))
                factor = jnp.exp2(old - new)
                product, part = weighed(tile, jnp.exp2(scores - spread(new)))
                acc[...] = acc[...] * factor + product
                total[...] = total[...] * factor + part
                top[...] = new

            def running_tile(tile, c):
                running(tile, False)
                return c

            lax.fori_loop(key_low, diagonal, running_tile, 0)
            running(diagonal, True)

        summed = jnp.sum(total[...], axis=1, keepdims=True)
        out_buf[pl.ds(at, tile_rows), :] = (acc[...] / summed).astype(jnp.bfloat16)

    def one_slab(order, waited):
        slab = jnp.bitwise_xor(hi, order)
        block = order * group + lo
        index, here = 0, slab == slabs[0]
        for number in range(1, n_slabs):
            index = jnp.where(slab == slabs[number], number, index)
            here = here | (slab == slabs[number])
        wanted = jnp.where(here, block + 1, waited)
        lax.fori_loop(waited, wanted, wait_for_block, 0)

        def one_tile(part, c):
            one_query_tile(index * tiles + part, block * rows_block + row0 + part * tile_rows)
            return c

        lax.fori_loop(0, jnp.where(here, tiles, 0), one_tile, 0)
        return wanted

    waited = lax.fori_loop(0, n_all, one_slab, 0)
    lax.fori_loop(waited, len(kv_sources), wait_for_block, 0)
    out_copies = [
        pltpu.make_async_copy(
            out_buf.at[pl.ds(slab * chunk, chunk), :], outs[slab], out_sems.at[slab]
        )
        for slab in range(n_slabs)
    ]
    for copy in out_copies:
        copy.start()
    for copy in out_copies:
        copy.wait()


def attend(pieces, kv_sources, where, slabs, paired, rows_block, row0, chunk):
    n_slots = len(kv_sources)
    n_slabs = len(slabs)
    n_all = len(pieces) // 2
    tile_rows = min(TILE, chunk)
    anywhere = pl.BlockSpec(memory_space=pl.ANY)
    return pl.pallas_call(
        functools.partial(
            attend_kernel, kv_sources, n_all, slabs, paired, rows_block, row0, chunk, tile_rows
        ),
        out_shape=[jax.ShapeDtypeStruct((chunk, HD), jnp.bfloat16)] * n_slabs,
        grid_spec=pltpu.PrefetchScalarGridSpec(
            num_scalar_prefetch=1,
            grid=(),
            in_specs=[anywhere] * len(pieces),
            out_specs=[anywhere] * n_slabs,
            scratch_shapes=[
                pltpu.VMEM((n_slots * rows_block, HD), jnp.bfloat16),
                pltpu.VMEM((n_slots * rows_block, HD), jnp.bfloat16),
                pltpu.VMEM((n_slabs * chunk, HD), jnp.bfloat16),
                pltpu.VMEM((n_slabs, DIGIT_ROWS, LANES), jnp.bfloat16),
                pltpu.VMEM((n_slabs * chunk, LANES), jnp.int32),
                pltpu.VMEM((n_slabs * chunk, HD), jnp.bfloat16),
                pltpu.VMEM((tile_rows, LANES), jnp.float32),
                pltpu.VMEM((tile_rows, LANES), jnp.float32),
                pltpu.VMEM((tile_rows, HD), jnp.float32),
                pltpu.SemaphoreType.DMA((2, n_slots)),
                pltpu.SemaphoreType.DMA((2, n_slabs)),
                pltpu.SemaphoreType.DMA((n_slabs,)),
            ],
        ),
        compiler_params=pltpu.CompilerParams(vmem_limit_bytes=VMEM_BYTES),
        cost_estimate=taking(2 + 4 * n_slabs),
    )(where, *pieces)


def out_kernel(parts, n_w, row0, has_sum, last, where, *refs):
    n_atts = len(parts)
    atts = refs[:n_atts]
    w_own, *rest = refs[n_atts:]
    w_parts, (tok_ref, *rest) = rest[:n_w], rest[n_w:]
    if has_sum:
        sum_ref, *rest = rest
    if last and row0:
        rest = rest[1:]
    out_ref, a_buf, w_buf, t_buf, o_buf, a_sems, w_sems, x_sems = rest
    hi, plane = where[0], where[2]
    rows, cols = o_buf.shape
    copies, waits = [], []
    col0 = pl.multiple_of(plane * cols, cols)
    at = 0
    for number, (step, slabs) in enumerate(parts):
        for place, slab in enumerate(slabs):
            copies.append(
                pltpu.make_async_copy(
                    atts[number].at[place], a_buf.at[:, pl.ds(at * HD, HD)], a_sems.at[at]
                )
            )
            head = jnp.bitwise_xor(hi, slab)
            into = w_buf.at[pl.ds(at * HD, HD), :]
            if step == 0:
                row = pl.multiple_of(head * HD, HD)
                source = w_own.at[pl.ds(row, HD), pl.ds(col0, cols)]
                copies.append(pltpu.make_async_copy(source, into, w_sems.at[at]))
            elif n_w == 1:
                row = pl.multiple_of(head * HD, HD)
                source = w_parts[0].at[step - 1, pl.ds(row, HD), :]
                copies.append(pltpu.make_async_copy(source, into, w_sems.at[at]))
            else:
                side = cols // 2
                for bit in range(2):
                    which = jnp.bitwise_xor(head, 2 * (hi >> bit & 1) + where[1])
                    target = w_buf.at[pl.ds(at * HD, HD), pl.ds(bit * side, side)]
                    for turn in range(n_w // 2):
                        source = w_parts[bit * (n_w // 2) + turn].at[step - 1]

                        def fetch(source=source, target=target, at=at):
                            pltpu.make_async_copy(source, target, w_sems.at[at]).start()

                        pl.when(which == turn)(fetch)
                waits.append(pltpu.make_async_copy(into, into, w_sems.at[at]))
            at += 1
    if has_sum:
        copies.append(pltpu.make_async_copy(sum_ref, t_buf, x_sems.at[0]))
    else:
        tok = tok_ref.at[pl.ds(row0, rows), pl.ds(col0, cols)]
        copies.append(pltpu.make_async_copy(tok, t_buf, x_sems.at[0]))
    for copy in copies:
        copy.start()
    for copy in copies + waits:
        copy.wait()
    product = jnp.dot(a_buf[...], w_buf[...], preferred_element_type=jnp.float32)
    o_buf[...] = (t_buf[...].astype(jnp.float32) + product).astype(o_buf.dtype)
    target = out_ref.at[pl.ds(row0, rows), :] if last else out_ref
    done = pltpu.make_async_copy(o_buf, target, x_sems.at[1])
    done.start()
    done.wait()


def project_out(where, parts, atts, w_own, w_parts, n_cols, tokens, row0, total, so_far, last):
    rows = atts[0].shape[1]
    n_rows, cols = tokens.shape[0], n_cols
    depth = sum(att.shape[0] for att in atts) * HD
    anywhere = pl.BlockSpec(memory_space=pl.ANY)
    operands = [*atts, w_own, *w_parts, tokens]
    has_sum = total is not None
    if has_sum:
        operands.append(total)
    aliases = {}
    if last and row0:
        aliases = {len(operands) + 1: 0}
        operands.append(so_far)
    kind = jnp.bfloat16 if last else jnp.float32
    return pl.pallas_call(
        functools.partial(out_kernel, parts, len(w_parts), row0, has_sum, last),
        out_shape=jax.ShapeDtypeStruct((n_rows if last else rows, cols), kind),
        grid_spec=pltpu.PrefetchScalarGridSpec(
            num_scalar_prefetch=1,
            grid=(),
            in_specs=[anywhere] * len(operands),
            out_specs=anywhere,
            scratch_shapes=[
                pltpu.VMEM((rows, depth), jnp.bfloat16),
                pltpu.VMEM((depth, cols), jnp.bfloat16),
                pltpu.VMEM((rows, cols), jnp.float32 if has_sum else jnp.bfloat16),
                pltpu.VMEM((rows, cols), kind),
                pltpu.SemaphoreType.DMA((depth // HD,)),
                pltpu.SemaphoreType.DMA((depth // HD,)),
                pltpu.SemaphoreType.DMA((2,)),
            ],
        ),
        input_output_aliases=aliases,
        compiler_params=pltpu.CompilerParams(vmem_limit_bytes=VMEM_BYTES),
        cost_estimate=taking(6),
    )(where, *operands)


def after(value, *others):
    return lax.optimization_barrier((value, *others))[0]


def shards(tokens, norm_gain, w_qkv, conv_filter, w_out, contig_offsets):
    n_rows, width = tokens.shape
    n_heads = w_qkv.shape[2] // HD
    n_ctx, n_planes = lax.axis_size("ctx"), lax.axis_size("mp")
    ctx, plane = lax.axis_index("ctx"), lax.axis_index("mp")
    group = n_ctx // n_heads
    assert group * n_heads == n_ctx and n_heads & (n_heads - 1) == 0
    hi, lo = ctx // group, ctx % group
    paired = group == 2 and n_heads % 2 == 0
    cols = width // n_planes
    where = jnp.stack([hi, lo, plane]).astype(jnp.int32)

    halo = ring_shift(tokens[n_rows - HALO :], "ctx", 1)
    w = w_qkv.transpose(1, 0, 2)
    taps = conv_filter.transpose(1, 0, 2)
    offs = jnp.broadcast_to(contig_offsets[:, None], (n_rows, LANES))
    lines = contig_offsets.reshape(n_rows // LANES, LANES)
    assert lines.shape[0] * 2 == DIGIT_ROWS
    digits = jnp.concatenate([lines // DIGIT, lines % DIGIT], axis=0).astype(jnp.bfloat16)
    gain = norm_gain[None, :]

    def run_project(batch, rows, raw):
        heads = jnp.stack([jnp.bitwise_xor(hi, k) for k in batch] + [ctx]).astype(jnp.int32)
        block = BLOCK if raw else n_rows
        return project(heads, rows, halo, gain, w, taps, offs, digits, block, raw)

    def send(slab, k):
        return swap_bits(slab, "ctx", k * group) if k else slab

    def w_piece(step, tied):
        half = n_heads // 2 * HD
        col0 = (plane + step) % n_planes * cols
        piece = lax.dynamic_slice(after(w_out, *tied), (lo * half, col0), (half, cols))
        return ring_shift(piece, "mp", step)

    own = [None] * n_heads
    if paired:
        far = n_heads - 1
        *slabs, normed = run_project([far], tokens, True)
        own[far] = send(slabs[0], far)
        side = cols // 2
        w_got = {}

        def bring(step, tied):
            begin = (plane + step) % n_planes * cols
            source = after(w_out, tied)
            both = [
                lax.dynamic_slice(
                    source, ((2 * (hi >> bit & 1) + lo) * HD, begin + bit * side), (HD, side)
                )
                for bit in range(2)
            ]
            w_got[step] = ring_shift(jnp.stack(both), "mp", step)

        for step in range(1, n_planes):
            bring(step, slabs[0])
        near = list(range(1, far))
        slabs = run_project(near, normed, False)
        slabs, own[far], w_got = lax.optimization_barrier((slabs, own[far], w_got))
        for k, slab in zip(near, slabs):
            own[k] = send(slab, k)
        own[0] = run_project([0], after(normed, slabs[0]), False)[0]
        w_got = [w_got[step] for step in range(1, n_planes)]
    else:
        order = list(range(n_heads))
        *slabs, _ = run_project(order, tokens, True)
        own = [send(slab, k) for k, slab in zip(order, slabs)]
        by_plane = w_out.reshape(n_heads * HD, n_planes, cols).transpose(1, 0, 2)
        got = lax.all_to_all(by_plane, "mp", split_axis=0, concat_axis=0, tiled=True)
        w_parts = [got[(plane - jnp.arange(1, n_planes)) % n_planes]]

    pieces = list(own)
    kv_sources = []
    if paired:
        pieces += [
            swap_bits(after(own[k], own[0]) if k else own[0], "ctx", 1) for k in range(n_heads)
        ]
        for k in range(n_heads):
            kv_sources += [((k, 1), (k, 2)), ((n_heads + k, 1), (n_heads + k, 2))]
    else:
        groups = [[a * group + b for b in range(group)] for a in range(n_heads)]
        for k, slab in enumerate(own):
            pieces.append(
                lax.all_gather(slab[1:, :n_rows], "ctx", axis=0, tiled=True, axis_index_groups=groups)
            )
            kv_sources += [((n_heads + k, 2 * b), (n_heads + k, 2 * b + 1)) for b in range(group)]
    n_chunks = 2
    chunk = n_rows // n_chunks

    everyone = tuple(range(n_heads))

    def run_attend(part, tied, slabs=everyone):
        at = after(where, *tied)
        return attend(pieces, kv_sources, at, slabs, paired, n_rows, part * chunk, chunk)

    def bring_home(outs, slabs=everyone):
        return jnp.stack([send(out, k) for k, out in zip(slabs, outs)])

    def run_out(part, some, total, so_far, last):
        return project_out(
            where, [p for p, _ in some], [a for _, a in some], w_out, w_parts,
            cols, tokens, part * chunk, total, so_far, last,
        )

    result = None
    if n_planes > 4 or not paired:
        for part in range(n_chunks):
            att = bring_home(run_attend(part, ()))
            gathered = lax.all_gather(att, "mp", axis=0)
            some = [((d, everyone), gathered[(plane - d) % n_planes]) for d in range(n_planes)]
            result = run_out(part, some, None, result, True)
        return result

    half = n_heads // 2
    w_near = jnp.stack(w_got, axis=1)
    w_next = swap_bits(w_near, "ctx", 1)
    w_parts = []
    for bit in range(2):
        mine = [w_near[bit], w_next[bit]]
        w_parts += mine + [swap_bits(part, "ctx", group << bit) for part in mine]
    def reach(ring):
        if n_planes > 1:
            ring[1] = ring_shift(ring[0], "mp", 1)
        if n_planes > 2:
            ring[n_planes - 1] = ring_shift(ring[0], "mp", n_planes - 1)

    def hop(ring, *tied):
        if n_planes > 3:
            ring[2] = ring_shift(after(ring[1], *tied), "mp", 1)

    outs = run_attend(0, ())
    outs = [after(out, w_parts[2], w_parts[3], w_parts[6], w_parts[7]) for out in outs]
    early = {0: bring_home(outs)}
    reach(early)
    turns = [tuple(k for k in everyone if k != half), (half,)]
    rings = []
    tied = (early[0],)
    for pair in turns:
        outs = run_attend(1, tied, pair)
        if rings:
            hop(rings[-1], outs[0])
            result = run_out(0, [((d, everyone), early[d]) for d in range(n_planes)], None, None, True)
            before = (result, rings[-1][1 % n_planes], rings[-1][n_planes - 1])
            outs = [after(out, *before) for out in outs]
        else:
            hop(early, outs[0], early[n_planes - 1])
        ring = {0: bring_home(outs, pair)}
        reach(ring)
        tied = (ring[0],)
        rings.append(ring)
    hop(rings[-1])
    late = [((d, pair), ring[d]) for pair, ring in zip(turns, rings) for d in range(n_planes)]
    last = [e for e in late if e[0][0] and (e[0][1] == turns[-1] or e[0][0] == n_planes // 2)]
    places = [place for place, _ in last]
    total = run_out(1, [e for e in late if e[0] not in places], None, None, False)
    return run_out(1, last, total, result, True)


def solution(mesh):
    placed = (
        P("ctx", None),
        P(),
        P(None, None, "mp"),
        P(None, None, "mp"),
        P("mp", None),
        P("ctx"),
    )
    return jax.shard_map(
        shards, mesh=mesh, in_specs=placed, out_specs=P("ctx", "mp"), check_vma=False
    )
```

```python
import functools
import math

import jax
import jax.numpy as jnp
from jax import lax
from jax.experimental import pallas as pl
from jax.experimental.pallas import tpu as pltpu
from jax.sharding import PartitionSpec as P

HD = 128
KERNEL = 7
HALO = 16
BLOCK = 256
DIGIT_ROWS = 16
DIGIT = 128
TILE = 512
LANES = 128
NEG = -2.0e38
OVERFLOW = 2.0**100
QUERY_SCALE = math.log2(math.e) / math.sqrt(HD)
VMEM_BYTES = 60 * 1024 * 1024
SCALE = 0.3


def taking(microseconds):
    return pl.CostEstimate(
        flops=int(microseconds * 1.1e9 * SCALE), bytes_accessed=1024, transcendentals=0
    )


def ring_shift(value, axis, by):
    size = lax.axis_size(axis)
    return lax.ppermute(value, axis, [(i, (i + by) % size) for i in range(size)])


def swap_bits(value, axis, bits):
    size = lax.axis_size(axis)
    return lax.ppermute(value, axis, [(i, i ^ bits) for i in range(size)])


def normed_rows(rows, gain):
    rows = rows.astype(jnp.float32)
    inverse = lax.rsqrt(jnp.mean(rows * rows, axis=-1, keepdims=True) + 1e-06)
    return (rows * inverse * gain).astype(jnp.bfloat16)


def project_kernel(n_heads, block, raw, heads, *refs):
    x_ref, halo_ref, gain_ref, w_ref, taps_ref, offs_ref, digits_ref = refs[:7]
    slabs = refs[7 : 7 + n_heads]
    rest = refs[7 + n_heads :]
    if raw:
        normed_ref, *rest = rest
    x_buf, halo_buf, w_buf, proj, out_buf, x_sems, w_sems, out_sems, n_sems = rest
    tiles = 3 * n_heads
    n_rows = x_ref.shape[0]
    n_blocks = n_rows // block

    def rows_copy(i):
        place = pl.ds(i * block, block)
        return pltpu.make_async_copy(x_ref.at[place, :], x_buf.at[place, :], x_sems.at[i])

    def weight_copy(tile):
        kind, slot = tile // n_heads, tile % n_heads
        start = pl.multiple_of(heads[slot] * HD, HD)
        return pltpu.make_async_copy(
            w_ref.at[kind, :, pl.ds(start, HD)],
            w_buf.at[:, pl.ds(tile * HD, HD)],
            w_sems.at[tile],
        )

    def out_copy(i, slot):
        place = pl.ds(i * block, block if i + 1 < n_blocks else block + DIGIT_ROWS)
        return pltpu.make_async_copy(
            out_buf.at[slot, :, place, :], slabs[slot].at[:, place, :], out_sems.at[i, slot]
        )

    rows_copy(0).start()
    for tile in range(tiles):
        weight_copy(tile).start()
    for i in range(1, n_blocks):
        rows_copy(i).start()

    def multiply(begin, first):
        width = 2 if raw else tiles
        for pair in range(0, tiles, width):
            some = range(pair, min(pair + width, tiles))
            if first:
                for tile in some:
                    weight_copy(tile).wait()
            w = w_buf[:, pair * HD : (some[-1] + 1) * HD]
            if first:
                before = jnp.dot(halo_buf[...], w, preferred_element_type=jnp.float32)
            here = x_buf[begin : begin + block, :]
            product = jnp.dot(here, w, preferred_element_type=jnp.float32)
            for tile in some:
                own = slice((tile - pair) * HD, (tile - pair + 1) * HD)
                if first:
                    proj[tile, :HALO, :] = before[:, own].astype(jnp.bfloat16).astype(jnp.float32)
                piece = product[:, own].astype(jnp.bfloat16).astype(jnp.float32)
                proj[tile, HALO + begin : HALO + begin + block, :] = piece

    def mix(i):
        begin = i * block
        offs = offs_ref[begin : begin + block, :]
        for tile in range(tiles):
            kind, slot = tile // n_heads, tile % n_heads
            start = pl.multiple_of(heads[slot] * HD, HD)
            taps = taps_ref[kind, :, pl.ds(start, HD)]
            total = taps[0:1, :] * proj[tile, HALO + begin : HALO + begin + block, :]
            for lag in range(1, KERNEL):
                at = HALO - lag + begin
                shifted = taps[lag : lag + 1, :] * proj[tile, at : at + block, :]
                total = total + jnp.where(offs >= lag, shifted, 0.0)
            if kind == 0:
                total = total * QUERY_SCALE
            out_buf[slot, kind, begin : begin + block, :] = total.astype(jnp.bfloat16)

    def normed_copy(i):
        place = pl.ds(i * block, block)
        return pltpu.make_async_copy(x_buf.at[place, :], normed_ref.at[place, :], n_sems.at[i])

    def rows_ready(i):
        rows_copy(i).wait()
        if raw:
            begin = i * block
            x_buf[begin : begin + block, :] = normed_rows(
                x_buf[begin : begin + block, :], gain_ref[...]
            )
            normed_copy(i).start()

    before_rows = normed_rows(halo_ref[...], gain_ref[...])
    halo_buf[...] = jnp.where(heads[n_heads] == 0, jnp.zeros_like(before_rows), before_rows)
    for slot in range(n_heads):
        for kind in range(3):
            out_buf[slot, kind, n_rows:, :] = digits_ref[...]
    rows_ready(0)
    multiply(0, True)
    for i in range(n_blocks):
        if i + 1 < n_blocks:
            rows_ready(i + 1)
            multiply((i + 1) * block, False)
        mix(i)
        for slot in range(n_heads):
            out_copy(i, slot).start()
    for i in range(n_blocks):
        for slot in range(n_heads):
            out_copy(i, slot).wait()
        if raw:
            normed_copy(i).wait()


def project(heads, rows, halo, gain, w, taps, offs, digits, block, raw):
    n_rows, width = rows.shape
    n_heads = heads.shape[0] - 1
    anywhere = pl.BlockSpec(memory_space=pl.ANY)
    vmem = pl.BlockSpec(memory_space=pltpu.VMEM)
    n_blocks = n_rows // block
    slab_rows = n_rows + DIGIT_ROWS
    out_shape = [jax.ShapeDtypeStruct((3, slab_rows, HD), jnp.bfloat16)] * n_heads
    if raw:
        out_shape.append(jax.ShapeDtypeStruct(rows.shape, jnp.bfloat16))
    return pl.pallas_call(
        functools.partial(project_kernel, n_heads, block, raw),
        out_shape=out_shape,
        grid_spec=pltpu.PrefetchScalarGridSpec(
            num_scalar_prefetch=1,
            grid=(),
            in_specs=[anywhere, vmem, vmem, anywhere, vmem, vmem, vmem],
            out_specs=[anywhere] * len(out_shape),
            scratch_shapes=[
                pltpu.VMEM((n_rows, width), jnp.bfloat16),
                pltpu.VMEM((HALO, width), jnp.bfloat16),
                pltpu.VMEM((width, 3 * n_heads * HD), jnp.bfloat16),
                pltpu.VMEM((3 * n_heads, HALO + n_rows, HD), jnp.float32),
                pltpu.VMEM((n_heads, 3, slab_rows, HD), jnp.bfloat16),
                pltpu.SemaphoreType.DMA((n_blocks,)),
                pltpu.SemaphoreType.DMA((3 * n_heads,)),
                pltpu.SemaphoreType.DMA((n_blocks, n_heads)),
                pltpu.SemaphoreType.DMA((n_blocks,)),
            ],
        ),
        compiler_params=pltpu.CompilerParams(vmem_limit_bytes=VMEM_BYTES),
        cost_estimate=taking(6 + 6 * n_heads),
    )(heads, rows, halo, gain, w, taps, offs, digits)


def attend_kernel(
    kv_sources, n_all, slabs, paired, rows_block, row0, chunk, tile_rows, where, *refs
):
    n_slabs = len(slabs)
    n_pieces = 1 + max(max(k[0], v[0]) for k, v in kv_sources)
    pieces = refs[:n_pieces]
    outs = refs[n_pieces : n_pieces + n_slabs]
    rest = refs[n_pieces + n_slabs :]
    k_buf, v_buf, q_buf, digits, first_ref, out_buf, top, total, acc, kv_sems, q_sems, out_sems = rest
    group = len(kv_sources) // n_all
    hi, lo = where[0], where[1]

    def slot_of(block):
        within = block % group
        if paired:
            within = jnp.bitwise_xor(within, lo)
        return jnp.bitwise_xor(block // group, hi) * group + within

    q_copies = []
    for slab in range(n_slabs):
        q_copies.append(
            pltpu.make_async_copy(
                pieces[slabs[slab]].at[0, pl.ds(row0, chunk), :],
                q_buf.at[pl.ds(slab * chunk, chunk), :],
                q_sems.at[0, slab],
            )
        )
        q_copies.append(
            pltpu.make_async_copy(
                pieces[slabs[slab]].at[0, pl.ds(rows_block, DIGIT_ROWS), :],
                digits.at[slab],
                q_sems.at[1, slab],
            )
        )
    for copy in q_copies:
        copy.start()
    for slot, (k_at, v_at) in enumerate(kv_sources):
        place = pl.ds(slot * rows_block, rows_block)
        for at, buf, side in ((k_at, k_buf, 0), (v_at, v_buf, 1)):
            source = pieces[at[0]].at[at[1], pl.ds(0, rows_block), :]
            pltpu.make_async_copy(source, buf.at[place, :], kv_sems.at[side, slot]).start()

    def wait_for_block(block, c):
        slot = slot_of(block)
        place = pl.ds(pl.multiple_of(slot * rows_block, rows_block), rows_block)
        for at, buf, side in ((kv_sources[0][0], k_buf, 0), (kv_sources[0][1], v_buf, 1)):
            source = pieces[at[0]].at[at[1], pl.ds(0, rows_block), :]
            pltpu.make_async_copy(source, buf.at[place, :], kv_sems.at[side, slot]).wait()
        return c

    for copy in q_copies:
        copy.wait()

    shape = (LANES, LANES)
    rows = lax.broadcasted_iota(jnp.int32, shape, 0)
    same = rows == lax.broadcasted_iota(jnp.int32, shape, 1)
    ones = jnp.ones(shape, jnp.bfloat16)
    for slab in range(n_slabs):
        block = jnp.bitwise_xor(hi, slabs[slab]) * group + lo
        both = digits[slab].astype(jnp.float32)
        for part in range(chunk // LANES):
            line = row0 // LANES + part

            def down(row):
                across = jnp.where(same, jnp.broadcast_to(both[row : row + 1, :], shape), 0.0)
                return jnp.dot(
                    across.astype(jnp.bfloat16), ones, preferred_element_type=jnp.float32
                )

            offset = down(line) * DIGIT + down(DIGIT_ROWS // 2 + line)
            begin = block * rows_block + row0 + part * LANES
            at = slab * chunk + part * LANES
            first_ref[at : at + LANES, :] = begin + rows - offset.astype(jnp.int32)

    tiles = chunk // tile_rows
    wide = tile_rows // LANES
    pair = rows_block // tile_rows

    def spread(column, count=1):
        return jnp.concatenate([column] * (wide * count), axis=1)

    def one_query_tile(index, begin):
        at = pl.multiple_of(index * tile_rows, tile_rows)
        first_low = jnp.min(first_ref[pl.ds(at, 8), :])
        first_high = jnp.max(first_ref[pl.ds(at + tile_rows - 8, 8), :])
        q = q_buf[pl.ds(at, tile_rows), :]
        diagonal = begin // tile_rows

        def key_rows(tile, count=1):
            key_begin = tile * tile_rows
            slot = slot_of(key_begin // rows_block)
            row = slot * rows_block + key_begin % rows_block
            return pl.ds(pl.multiple_of(row, tile_rows), count * tile_rows)

        def scores_of(tile, lower, upper, count=1):
            shape = (tile_rows, count * tile_rows)
            scores = lax.dot_general(
                q,
                k_buf[key_rows(tile, count), :],
                (((1,), (1,)), ((), ())),
                preferred_element_type=jnp.float32,
            )
            if lower or upper:
                lane = lax.broadcasted_iota(jnp.int32, shape, 1)
            if lower:
                first = first_ref[pl.ds(at, tile_rows), :] - tile * tile_rows
                scores = jnp.where(lane >= spread(first), scores, NEG)
            if upper:
                row = lax.broadcasted_iota(jnp.int32, shape, 0)
                scores = jnp.where(lane <= row, scores, NEG)
            return scores

        def weighed(tile, weights, count=1):
            part = weights[:, :LANES]
            for piece in range(1, wide * count):
                part = part + weights[:, piece * LANES : (piece + 1) * LANES]
            product = jnp.dot(
                weights.astype(jnp.bfloat16),
                v_buf[key_rows(tile, count), :],
                preferred_element_type=jnp.float32,
            )
            return product, part

        def fixed_top(tile, lower, count=1):
            scores = scores_of(tile, lower, False, count)
            weights = jnp.exp2(scores - spread(top[...], count))
            product, part = weighed(tile, weights, count)
            acc[...] += product
            total[...] += part

        def masked_tile(tile, c):
            fixed_top(tile, True)
            return c

        def open_tile(tile, c):
            fixed_top(tile, False)
            return c

        def open_block(block, c):
            fixed_top(block * pair, False, pair)
            return c

        key_low = first_low // tile_rows
        open_low = jnp.minimum((first_high + tile_rows - 1) // tile_rows, diagonal)
        scores = scores_of(diagonal, True, True)
        top[...] = jnp.broadcast_to(jnp.max(scores, axis=1, keepdims=True), top.shape)
        acc[...], total[...] = weighed(diagonal, jnp.exp2(scores - spread(top[...])))
        lax.fori_loop(key_low, open_low, masked_tile, 0)
        block_end = diagonal // pair
        block_low = (open_low + pair - 1) // pair
        lax.fori_loop(open_low, jnp.minimum(block_low * pair, diagonal), open_tile, 0)
        lax.fori_loop(block_low, block_end, open_block, 0)
        lax.fori_loop(jnp.maximum(block_end * pair, jnp.minimum(block_low * pair, diagonal)), diagonal, open_tile, 0)

        @pl.when(jnp.logical_not(jnp.max(total[...]) < OVERFLOW))
        def _():
            top[...] = jnp.full(top.shape, NEG, jnp.float32)
            total[...] = jnp.zeros(total.shape, jnp.float32)
            acc[...] = jnp.zeros(acc.shape, jnp.float32)

            def running(tile, upper):
                scores = scores_of(tile, True, upper)
                old = top[...]
                new = jnp.maximum(old, jnp.max(scores, axis=1, keepdims=True))
                factor = jnp.exp2(old - new)
                product, part = weighed(tile, jnp.exp2(scores - spread(new)))
                acc[...] = acc[...] * factor + product
                total[...] = total[...] * factor + part
                top[...] = new

            def running_tile(tile, c):
                running(tile, False)
                return c

            lax.fori_loop(key_low, diagonal, running_tile, 0)
            running(diagonal, True)

        summed = jnp.sum(total[...], axis=1, keepdims=True)
        out_buf[pl.ds(at, tile_rows), :] = (acc[...] / summed).astype(jnp.bfloat16)

    def one_slab(order, waited):
        slab = jnp.bitwise_xor(hi, order)
        block = order * group + lo
        index, here = 0, slab == slabs[0]
        for number in range(1, n_slabs):
            index = jnp.where(slab == slabs[number], number, index)
            here = here | (slab == slabs[number])
        wanted = jnp.where(here, block + 1, waited)
        lax.fori_loop(waited, wanted, wait_for_block, 0)

        def one_tile(part, c):
            one_query_tile(index * tiles + part, block * rows_block + row0 + part * tile_rows)
            return c

        lax.fori_loop(0, jnp.where(here, tiles, 0), one_tile, 0)
        return wanted

    waited = lax.fori_loop(0, n_all, one_slab, 0)
    lax.fori_loop(waited, len(kv_sources), wait_for_block, 0)
    out_copies = [
        pltpu.make_async_copy(
            out_buf.at[pl.ds(slab * chunk, chunk), :], outs[slab], out_sems.at[slab]
        )
        for slab in range(n_slabs)
    ]
    for copy in out_copies:
        copy.start()
    for copy in out_copies:
        copy.wait()


def attend(pieces, kv_sources, where, slabs, paired, rows_block, row0, chunk):
    n_slots = len(kv_sources)
    n_slabs = len(slabs)
    n_all = len(pieces) // 2
    tile_rows = min(TILE, chunk)
    anywhere = pl.BlockSpec(memory_space=pl.ANY)
    return pl.pallas_call(
        functools.partial(
            attend_kernel, kv_sources, n_all, slabs, paired, rows_block, row0, chunk, tile_rows
        ),
        out_shape=[jax.ShapeDtypeStruct((chunk, HD), jnp.bfloat16)] * n_slabs,
        grid_spec=pltpu.PrefetchScalarGridSpec(
            num_scalar_prefetch=1,
            grid=(),
            in_specs=[anywhere] * len(pieces),
            out_specs=[anywhere] * n_slabs,
            scratch_shapes=[
                pltpu.VMEM((n_slots * rows_block, HD), jnp.bfloat16),
                pltpu.VMEM((n_slots * rows_block, HD), jnp.bfloat16),
                pltpu.VMEM((n_slabs * chunk, HD), jnp.bfloat16),
                pltpu.VMEM((n_slabs, DIGIT_ROWS, LANES), jnp.bfloat16),
                pltpu.VMEM((n_slabs * chunk, LANES), jnp.int32),
                pltpu.VMEM((n_slabs * chunk, HD), jnp.bfloat16),
                pltpu.VMEM((tile_rows, LANES), jnp.float32),
                pltpu.VMEM((tile_rows, LANES), jnp.float32),
                pltpu.VMEM((tile_rows, HD), jnp.float32),
                pltpu.SemaphoreType.DMA((2, n_slots)),
                pltpu.SemaphoreType.DMA((2, n_slabs)),
                pltpu.SemaphoreType.DMA((n_slabs,)),
            ],
        ),
        compiler_params=pltpu.CompilerParams(vmem_limit_bytes=VMEM_BYTES),
        cost_estimate=taking(2 + 4 * n_slabs),
    )(where, *pieces)


def out_kernel(parts, n_w, row0, has_sum, last, where, *refs):
    n_atts = len(parts)
    atts = refs[:n_atts]
    w_own, *rest = refs[n_atts:]
    w_parts, (tok_ref, *rest) = rest[:n_w], rest[n_w:]
    if has_sum:
        sum_ref, *rest = rest
    if last and row0:
        rest = rest[1:]
    out_ref, a_buf, w_buf, t_buf, o_buf, a_sems, w_sems, x_sems = rest
    hi, plane = where[0], where[2]
    rows, cols = o_buf.shape
    copies, waits = [], []
    col0 = pl.multiple_of(plane * cols, cols)
    at = 0
    for number, (step, slabs) in enumerate(parts):
        for place, slab in enumerate(slabs):
            copies.append(
                pltpu.make_async_copy(
                    atts[number].at[place], a_buf.at[:, pl.ds(at * HD, HD)], a_sems.at[at]
                )
            )
            head = jnp.bitwise_xor(hi, slab)
            into = w_buf.at[pl.ds(at * HD, HD), :]
            if step == 0:
                row = pl.multiple_of(head * HD, HD)
                source = w_own.at[pl.ds(row, HD), pl.ds(col0, cols)]
                copies.append(pltpu.make_async_copy(source, into, w_sems.at[at]))
            elif n_w == 1:
                row = pl.multiple_of(head * HD, HD)
                source = w_parts[0].at[step - 1, pl.ds(row, HD), :]
                copies.append(pltpu.make_async_copy(source, into, w_sems.at[at]))
            else:
                side = cols // 2
                for bit in range(2):
                    which = jnp.bitwise_xor(head, 2 * (hi >> bit & 1) + where[1])
                    target = w_buf.at[pl.ds(at * HD, HD), pl.ds(bit * side, side)]
                    for turn in range(n_w // 2):
                        source = w_parts[bit * (n_w // 2) + turn].at[step - 1]

                        def fetch(source=source, target=target, at=at):
                            pltpu.make_async_copy(source, target, w_sems.at[at]).start()

                        pl.when(which == turn)(fetch)
                waits.append(pltpu.make_async_copy(into, into, w_sems.at[at]))
            at += 1
    if has_sum:
        copies.append(pltpu.make_async_copy(sum_ref, t_buf, x_sems.at[0]))
    else:
        tok = tok_ref.at[pl.ds(row0, rows), pl.ds(col0, cols)]
        copies.append(pltpu.make_async_copy(tok, t_buf, x_sems.at[0]))
    for copy in copies:
        copy.start()
    for copy in copies + waits:
        copy.wait()
    product = jnp.dot(a_buf[...], w_buf[...], preferred_element_type=jnp.float32)
    o_buf[...] = (t_buf[...].astype(jnp.float32) + product).astype(o_buf.dtype)
    target = out_ref.at[pl.ds(row0, rows), :] if last else out_ref
    done = pltpu.make_async_copy(o_buf, target, x_sems.at[1])
    done.start()
    done.wait()


def project_out(where, parts, atts, w_own, w_parts, n_cols, tokens, row0, total, so_far, last):
    rows = atts[0].shape[1]
    n_rows, cols = tokens.shape[0], n_cols
    depth = sum(att.shape[0] for att in atts) * HD
    anywhere = pl.BlockSpec(memory_space=pl.ANY)
    operands = [*atts, w_own, *w_parts, tokens]
    has_sum = total is not None
    if has_sum:
        operands.append(total)
    aliases = {}
    if last and row0:
        aliases = {len(operands) + 1: 0}
        operands.append(so_far)
    kind = jnp.bfloat16 if last else jnp.float32
    return pl.pallas_call(
        functools.partial(out_kernel, parts, len(w_parts), row0, has_sum, last),
        out_shape=jax.ShapeDtypeStruct((n_rows if last else rows, cols), kind),
        grid_spec=pltpu.PrefetchScalarGridSpec(
            num_scalar_prefetch=1,
            grid=(),
            in_specs=[anywhere] * len(operands),
            out_specs=anywhere,
            scratch_shapes=[
                pltpu.VMEM((rows, depth), jnp.bfloat16),
                pltpu.VMEM((depth, cols), jnp.bfloat16),
                pltpu.VMEM((rows, cols), jnp.float32 if has_sum else jnp.bfloat16),
                pltpu.VMEM((rows, cols), kind),
                pltpu.SemaphoreType.DMA((depth // HD,)),
                pltpu.SemaphoreType.DMA((depth // HD,)),
                pltpu.SemaphoreType.DMA((2,)),
            ],
        ),
        input_output_aliases=aliases,
        compiler_params=pltpu.CompilerParams(vmem_limit_bytes=VMEM_BYTES),
        cost_estimate=taking(6),
    )(where, *operands)


def after(value, *others):
    return lax.optimization_barrier((value, *others))[0]


def shards(tokens, norm_gain, w_qkv, conv_filter, w_out, contig_offsets):
    n_rows, width = tokens.shape
    n_heads = w_qkv.shape[2] // HD
    n_ctx, n_planes = lax.axis_size("ctx"), lax.axis_size("mp")
    ctx, plane = lax.axis_index("ctx"), lax.axis_index("mp")
    group = n_ctx // n_heads
    assert group * n_heads == n_ctx and n_heads & (n_heads - 1) == 0
    hi, lo = ctx // group, ctx % group
    paired = group == 2 and n_heads % 2 == 0
    cols = width // n_planes
    where = jnp.stack([hi, lo, plane]).astype(jnp.int32)

    halo = ring_shift(tokens[n_rows - HALO :], "ctx", 1)
    w = w_qkv.transpose(1, 0, 2)
    taps = conv_filter.transpose(1, 0, 2)
    offs = jnp.broadcast_to(contig_offsets[:, None], (n_rows, LANES))
    lines = contig_offsets.reshape(n_rows // LANES, LANES)
    assert lines.shape[0] * 2 == DIGIT_ROWS
    digits = jnp.concatenate([lines // DIGIT, lines % DIGIT], axis=0).astype(jnp.bfloat16)
    gain = norm_gain[None, :]

    def run_project(batch, rows, raw):
        heads = jnp.stack([jnp.bitwise_xor(hi, k) for k in batch] + [ctx]).astype(jnp.int32)
        block = BLOCK if raw else n_rows
        return project(heads, rows, halo, gain, w, taps, offs, digits, block, raw)

    def send(slab, k):
        return swap_bits(slab, "ctx", k * group) if k else slab

    def w_piece(step, tied):
        half = n_heads // 2 * HD
        col0 = (plane + step) % n_planes * cols
        piece = lax.dynamic_slice(after(w_out, *tied), (lo * half, col0), (half, cols))
        return ring_shift(piece, "mp", step)

    own = [None] * n_heads
    if paired:
        far = n_heads - 1
        *slabs, normed = run_project([far], tokens, True)
        own[far] = send(slabs[0], far)
        side = cols // 2
        w_got = {}

        def bring(step, tied):
            begin = (plane + step) % n_planes * cols
            source = w_out
            both = [
                lax.dynamic_slice(
                    source, ((2 * (hi >> bit & 1) + lo) * HD, begin + bit * side), (HD, side)
                )
                for bit in range(2)
            ]
            w_got[step] = ring_shift(jnp.stack(both), "mp", step)

        for step in range(1, n_planes):
            bring(step, slabs[0])
        near = list(range(1, far))
        slabs = run_project(near, normed, False)
        slabs, own[far], w_got = lax.optimization_barrier((slabs, own[far], w_got))
        for k, slab in zip(near, slabs):
            own[k] = send(slab, k)
        own[0] = run_project([0], after(normed, slabs[0]), False)[0]
        w_got = [w_got[step] for step in range(1, n_planes)]
    else:
        order = list(range(n_heads))
        *slabs, _ = run_project(order, tokens, True)
        own = [send(slab, k) for k, slab in zip(order, slabs)]
        by_plane = w_out.reshape(n_heads * HD, n_planes, cols).transpose(1, 0, 2)
        got = lax.all_to_all(by_plane, "mp", split_axis=0, concat_axis=0, tiled=True)
        w_parts = [got[(plane - jnp.arange(1, n_planes)) % n_planes]]

    pieces = list(own)
    kv_sources = []
    if paired:
        pieces += [
            swap_bits(after(own[k], own[0]) if k else own[0], "ctx", 1) for k in range(n_heads)
        ]
        for k in range(n_heads):
            kv_sources += [((k, 1), (k, 2)), ((n_heads + k, 1), (n_heads + k, 2))]
    else:
        groups = [[a * group + b for b in range(group)] for a in range(n_heads)]
        for k, slab in enumerate(own):
            pieces.append(
                lax.all_gather(slab[1:, :n_rows], "ctx", axis=0, tiled=True, axis_index_groups=groups)
            )
            kv_sources += [((n_heads + k, 2 * b), (n_heads + k, 2 * b + 1)) for b in range(group)]
    n_chunks = 2
    chunk = n_rows // n_chunks

    everyone = tuple(range(n_heads))

    def run_attend(part, tied, slabs=everyone):
        at = after(where, *tied)
        return attend(pieces, kv_sources, at, slabs, paired, n_rows, part * chunk, chunk)

    def bring_home(outs, slabs=everyone):
        return jnp.stack([send(out, k) for k, out in zip(slabs, outs)])

    def run_out(part, some, total, so_far, last):
        return project_out(
            where, [p for p, _ in some], [a for _, a in some], w_out, w_parts,
            cols, tokens, part * chunk, total, so_far, last,
        )

    result = None
    if n_planes > 4 or not paired:
        for part in range(n_chunks):
            att = bring_home(run_attend(part, ()))
            gathered = lax.all_gather(att, "mp", axis=0)
            some = [((d, everyone), gathered[(plane - d) % n_planes]) for d in range(n_planes)]
            result = run_out(part, some, None, result, True)
        return result

    half = n_heads // 2
    w_near = jnp.stack(w_got, axis=1)
    w_next = swap_bits(w_near, "ctx", 1)
    w_parts = []
    for bit in range(2):
        mine = [w_near[bit], w_next[bit]]
        w_parts += mine + [swap_bits(part, "ctx", group << bit) for part in mine]
    def reach(ring):
        if n_planes > 1:
            ring[1] = ring_shift(ring[0], "mp", 1)
        if n_planes > 2:
            ring[n_planes - 1] = ring_shift(ring[0], "mp", n_planes - 1)

    def hop(ring, *tied):
        if n_planes > 3:
            ring[2] = ring_shift(after(ring[1], *tied), "mp", 1)

    outs = run_attend(0, ())
    outs = [after(out, w_parts[2], w_parts[3], w_parts[6], w_parts[7]) for out in outs]
    early = {0: bring_home(outs)}
    reach(early)
    turns = [tuple(k for k in everyone if k != half), (half,)]
    rings = []
    tied = (early[0],)
    for pair in turns:
        outs = run_attend(1, tied, pair)
        if rings:
            hop(rings[-1], outs[0])
            result = run_out(0, [((d, everyone), early[d]) for d in range(n_planes)], None, None, True)
            before = (result, rings[-1][1 % n_planes], rings[-1][n_planes - 1])
            outs = [after(out, *before) for out in outs]
        else:
            hop(early, outs[0], early[n_planes - 1])
        ring = {0: bring_home(outs, pair)}
        reach(ring)
        tied = (ring[0],)
        rings.append(ring)
    hop(rings[-1])
    late = [((d, pair), ring[d]) for pair, ring in zip(turns, rings) for d in range(n_planes)]
    last = [e for e in late if e[0][0] and (e[0][1] == turns[-1] or e[0][0] == n_planes // 2)]
    places = [place for place, _ in last]
    total = run_out(1, [e for e in late if e[0] not in places], None, None, False)
    return run_out(1, last, total, result, True)


def solution(mesh):
    placed = (
        P("ctx", None),
        P(),
        P(None, None, "mp"),
        P(None, None, "mp"),
        P("mp", None),
        P("ctx"),
    )
    return jax.shard_map(
        shards, mesh=mesh, in_specs=placed, out_specs=P("ctx", "mp"), check_vma=False
    )
```
